32 devices in a mesh: group: 2 (over y), line: 16 (over z, x, core).
Axes of the slice: x: 2, y: 2, z: 4, core: 2. Of those that a mesh axis runs over, the one named last changes fastest.
Arguments:
- residual_in: bfloat16 [2048, 2048], P(('group', 'line')), parts along dimension 0, may hold values from -6 to 6
- queries: bfloat16 [2048, 2048], P(('group', 'line')), parts along dimension 0, may hold values from -8 to 8
- question_key_values: bfloat16 [2048, 512], P(('group', 'line')), parts along dimension 0, may hold values from -8 to 8
- document_prefix_cache: bfloat16 [4096, 512], P(('group', 'line')), parts along dimension 0, may hold values from -8 to 8
- out_proj: bfloat16 [2048, 2048], P('line'), may hold values from -0.125 to 0.125
- norm_gain: float32 [2048], replicated, may hold values from 0.5 to 1.5
- routes: int32 [2048, 8], P(('group', 'line')), parts along dimension 0, may hold values from 0 to 15, all different within a row; in each aligned block of 32 rows (0 to 31, 32 to 63, ...) at most 32 rows name the same one
- keep_mask: int32 [2048, 8], P(('group', 'line')), parts along dimension 0, may hold values 0 or 1
- route_weights: float32 [2048, 8], P(('group', 'line')), parts along dimension 0, may hold values from 0.02 to 0.4
- expert_slots: int32 [16], replicated, may hold values from 0 to 15, each once
- expert_gate: bfloat16 [16, 2048, 768], P('line'), may hold values from -0.125 to 0.125
- expert_up: bfloat16 [16, 2048, 768], P('line'), may hold values from -0.125 to 0.125
- expert_down: bfloat16 [16, 768, 2048], P('line'), may hold values from -0.21875 to 0.21875
Outputs:
- layer_out: bfloat16 [2048, 2048], P(('group', 'line')), parts along dimension 0
The draws below stay inside these ranges and needn't reach their ends.
There are 2 independent parts, one for each index of `group`. The reference program is written for one: setup_inputs(seed, part) draws one part's arguments, and reference() takes and returns one part's arrays. A program takes and returns all parts, laid end to end along the dimension named above; an argument that names none is the same for every part. Nothing has to cross between parts.
Inputs may be any that keep to these rules, and one draw needn't show every extreme that they name: `routes`: each row names 8 different experts; in every aligned block of half of 64 rows no expert is named by more than 32 rows. `expert_slots`: every slot holds exactly one expert.
All inputs are finite; a program needn't handle non-finite values. No bound on the sum of `keep_mask` on one device may be relied on, other than what follows from the above.
Results may differ from the reference program's by a relative error of at most 0.0045.
Values may be sent and summed in bfloat16 or wider, within the bound.
A program may use at most 256 MiB of HBM per device.

```python
import math
import jax
import jax.numpy as jnp
import numpy as np
from jax import lax

D = 2048
QUERY_HEADS = 16
KEY_VALUE_HEADS = 2
HEAD_SIZE = 128
FF = 768
TOPK = 8
QLEN = 16
TOKENS_PER_LINE = 64
TOKEN_TOTAL = 1024
PREFIX_LENGTH = 2048
EXPERTS = 16
HCAP = 32


def draw_document_prefix_cache(key, part):
    key_portion, value_portion = jax.random.split(jax.random.fold_in(key, 5))
    key_matrix = jnp.clip(jax.random.normal(key_portion, (PREFIX_LENGTH, KEY_VALUE_HEADS, HEAD_SIZE), jnp.float32), -6.0, 6.0)
    value_matrix = jnp.clip(jax.random.normal(value_portion, (PREFIX_LENGTH, KEY_VALUE_HEADS, HEAD_SIZE), jnp.float32), -6.0, 6.0)
    return jnp.concatenate([key_matrix.reshape(PREFIX_LENGTH, KEY_VALUE_HEADS * HEAD_SIZE), value_matrix.reshape(PREFIX_LENGTH, KEY_VALUE_HEADS * HEAD_SIZE)], axis=1).astype(jnp.bfloat16)


def draw_queries(key, part):
    base_key = jax.random.fold_in(key, 9)
    query_table = jnp.clip(2.0 * jax.random.normal(base_key, (TOKEN_TOTAL, QUERY_HEADS * HEAD_SIZE), jnp.float32), -8.0, 8.0)
    return query_table.astype(jnp.bfloat16)


def draw_question_key_values(key, part):
    key_portion, value_portion = jax.random.split(jax.random.fold_in(key, 13))
    key_matrix = jnp.clip(1.6 * jax.random.normal(key_portion, (TOKEN_TOTAL, KEY_VALUE_HEADS * HEAD_SIZE), jnp.float32), -8.0, 8.0)
    value_matrix = jnp.clip(jax.random.normal(value_portion, (TOKEN_TOTAL, KEY_VALUE_HEADS * HEAD_SIZE), jnp.float32), -6.0, 6.0)
    return jnp.concatenate([key_matrix, value_matrix], axis=1).astype(jnp.bfloat16)


def touch_ends(values, stream_key, smallest, largest):
    shape = values.shape
    place = [jax.random.randint(jax.random.fold_in(stream_key, axis), (), 0, shape[axis]) for axis in range(len(shape))]
    values = values.at[tuple(place)].set(smallest)
    longest = shape.index(max(shape))
    place[longest] = (place[longest] + 1) % shape[longest]
    return values.at[tuple(place)].set(largest)


def shard_levels(own_key, shape, cuts, smallest, high):
    level, own = 1.0, jax.random.fold_in(own_key, 6)
    for dim, blocks in cuts:
        steps = jnp.exp(jax.random.uniform(jax.random.fold_in(own, dim), (blocks,), jnp.float32, smallest / len(cuts), high / len(cuts)))
        level = level * jnp.repeat(steps, shape[dim] // blocks).reshape([-1 if axis == dim else 1 for axis in range(len(shape))])
    return level


def shared_out(key, own, number, rows, amount, top, bound, skew):
    sequence = jax.random.permutation(key, amount)
    packed, common = shares(amount, rows * top, bound, skew, True), shares(amount, rows * top, bound, skew, False)
    places = jnp.arange(amount)

    def named(tallies, turn):
        used = int((tallies > 0).sum())
        fixed = max(1, used // 4)
        passed = fixed + (places - fixed + turn * (used - fixed)) % max(1, amount - fixed)
        return jnp.zeros((amount,), jnp.int32).at[sequence[jnp.where(places < fixed, places, passed)]].set(jnp.asarray(tallies, jnp.int32))

    tallies = jnp.where(number % 4 == 0, named(packed, number // 4), named(common, number - number // 4 - 1))
    mixed = jax.random.permutation(jax.random.fold_in(own, 3), amount)
    donor, sink = mixed[0:amount // 2 * 2:2], mixed[1:amount // 2 * 2:2]
    margin = jnp.minimum(tallies[donor] - 1, bound - tallies[sink]) // 2
    margin = jnp.where((donor == sequence[0]) | (sink == sequence[0]) | (tallies[sink] == 0), 0, jnp.maximum(margin, 0))
    passed = jax.random.randint(jax.random.fold_in(own, 4), (amount // 2,), 0, 1 << 20) % (margin + 1)
    tallies = tallies.at[donor].add(-passed).at[sink].add(passed)
    items = jnp.searchsorted(jnp.cumsum(tallies), jnp.arange(rows * top), side="right").astype(jnp.int32)
    listing = items.reshape(top, rows).T
    listing = listing[jax.random.permutation(jax.random.fold_in(own, 1), rows)]
    turn = jax.random.randint(jax.random.fold_in(own, 2), (rows, 1), 0, top)
    return jnp.take_along_axis(listing, (jnp.arange(top)[None, :] + turn) % top, axis=1)


def shares(number_of, total, bound, slope, full):
    portions = [(1 << 20) // math.isqrt(grade ** slope) + 1 for grade in range(1, number_of + 1)]
    largest = bound if full else min(bound, max(-(-total // number_of), total * portions[0] // sum(portions)))
    least = 1 if total - largest >= number_of - 1 else 0
    given, surplus = [largest] + [least] * (number_of - 1), total - largest - least * (number_of - 1)
    while surplus > 0:
        free = [i for i in range(1, number_of) if given[i] < largest] or [i for i in range(1, number_of) if given[i] < bound]
        mass, budget = sum([portions[i] for i in free]), surplus
        for i in free:
            addition = min(bound - given[i], max(1, budget * portions[i] // mass), surplus)
            given[i] = given[i] + addition
            surplus = surplus - addition
    return np.array(given)


def normal_values(key, dims, width, most, pieces=(), kind=jnp.bfloat16):
    result = jax.random.normal(key, dims, jnp.float32) * width
    if len(pieces) > 0:
        result = shard_levels(key, dims, pieces, -0.22, 0.18) * result
    return jnp.clip(result, min=-most, max=most).astype(kind)


def setup_inputs(seed: int = 0, part: int = 0) -> dict:
    seeds = jax.random.split(jax.random.key(seed), 14)
    part_keys = jax.random.split(jax.random.fold_in(seeds[13], part), 14)
    residual_in = normal_values(part_keys[0], (TOKEN_TOTAL, D), 1.0, 6.0, ((0, 16),))
    queries = draw_queries(jax.random.fold_in(jax.random.fold_in(seeds[13], part), 71), part)
    question_key_values = draw_question_key_values(jax.random.fold_in(jax.random.fold_in(seeds[13], part), 71), part)
    document_prefix_cache = draw_document_prefix_cache(jax.random.fold_in(jax.random.fold_in(seeds[13], part), 71), part)
    out_proj = normal_values(seeds[4], (QUERY_HEADS * HEAD_SIZE, D), (QUERY_HEADS * HEAD_SIZE) ** -0.5, 0.125, ((0, 16),))
    norm_gain = jnp.clip(1.0 + 0.1 * jax.random.normal(seeds[5], (D,), jnp.float32), 0.5, 1.5)
    routes_keys = jax.random.split(jax.random.fold_in(part_keys[6], 1), TOKEN_TOTAL // (TOKENS_PER_LINE // 2))
    routes_turns = jax.random.permutation(jax.random.fold_in(part_keys[6], 3), TOKEN_TOTAL // (TOKENS_PER_LINE // 2))
    routes = jax.vmap(lambda own, number: shared_out(jax.random.fold_in(part_keys[6], 2), own, number, TOKENS_PER_LINE // 2, EXPERTS, TOPK, HCAP, 2))(routes_keys, routes_turns).reshape((TOKEN_TOTAL, TOPK))
    keep_mask = touch_ends((jax.random.randint(part_keys[7], (TOKEN_TOTAL, TOPK), 0, 4) < 3).astype(jnp.int32), jax.random.fold_in(part_keys[7], 1), 0, 1)
    route_weights = jnp.clip(jnp.exp(math.log(0.4) - 2.9957323 * jax.random.uniform(part_keys[8], (TOKEN_TOTAL, TOPK), jnp.float32) ** shard_levels(part_keys[8], (TOKEN_TOTAL, TOPK), ((0, 16),), -0.2, 0.2)), 0.02, 0.4)
    expert_slots = jax.random.permutation(seeds[9], EXPERTS).astype(jnp.int32)
    expert_gate = normal_values(seeds[10], (EXPERTS, D, FF), D ** -0.5, 0.125, ((0, 16),))
    expert_up = normal_values(seeds[11], (EXPERTS, D, FF), D ** -0.5, 0.125, ((0, 16),))
    expert_down = normal_values(seeds[12], (EXPERTS, FF, D), FF ** -0.5, 0.21875, ((0, 16),))
    return {"residual_in": residual_in, "queries": queries, "question_key_values": question_key_values, "document_prefix_cache": document_prefix_cache, "out_proj": out_proj, "norm_gain": norm_gain, "routes": routes, "keep_mask": keep_mask, "route_weights": route_weights, "expert_slots": expert_slots, "expert_gate": expert_gate, "expert_up": expert_up, "expert_down": expert_down}


def block_attention(paired_blocks, document_keys, document_values, visible_mask):
    queries_per_key_head = QUERY_HEADS // KEY_VALUE_HEADS
    score_scale = 1.0 / math.sqrt(HEAD_SIZE)
    block_of_queries, local_block = paired_blocks
    heads_of_queries = block_of_queries.reshape(TOKENS_PER_LINE, KEY_VALUE_HEADS, queries_per_key_head, HEAD_SIZE).astype(jnp.float32)
    local_keys = local_block[:, :KEY_VALUE_HEADS * HEAD_SIZE].reshape(TOKENS_PER_LINE, KEY_VALUE_HEADS, HEAD_SIZE).astype(jnp.float32)
    local_values = local_block[:, KEY_VALUE_HEADS * HEAD_SIZE:].reshape(TOKENS_PER_LINE, KEY_VALUE_HEADS, HEAD_SIZE).astype(jnp.float32)
    far_scores = jnp.einsum('thgd,nhd->thgn', heads_of_queries, document_keys) * score_scale
    near_scores = jnp.einsum('thgd,shd->thgs', heads_of_queries, local_keys) * score_scale
    near_scores = jnp.where(visible_mask[:, None, None, :], near_scores, -1e+30)
    row_max = jnp.maximum(far_scores.max(-1), near_scores.max(-1))
    far_terms = jnp.exp(far_scores - row_max[..., None])
    near_terms = jnp.exp(near_scores - row_max[..., None])
    denominator = far_terms.sum(-1) + near_terms.sum(-1)
    far_probs = lax.optimization_barrier(far_terms.astype(jnp.bfloat16)).astype(jnp.float32)
    near_probs = lax.optimization_barrier(near_terms.astype(jnp.bfloat16)).astype(jnp.float32)
    summed = jnp.einsum('thgn,nhd->thgd', far_probs, document_values) + jnp.einsum('thgs,shd->thgd', near_probs, local_values)
    return (summed / denominator[..., None]).reshape(TOKENS_PER_LINE, QUERY_HEADS * HEAD_SIZE).astype(jnp.bfloat16)

def reference(residual_in, queries, question_key_values, document_prefix_cache, out_proj, norm_gain, routes, keep_mask, route_weights, expert_slots, expert_gate, expert_up, expert_down):
    document_keys = document_prefix_cache[:, :KEY_VALUE_HEADS * HEAD_SIZE].reshape(PREFIX_LENGTH, KEY_VALUE_HEADS, HEAD_SIZE).astype(jnp.float32)
    document_values = document_prefix_cache[:, KEY_VALUE_HEADS * HEAD_SIZE:].reshape(PREFIX_LENGTH, KEY_VALUE_HEADS, HEAD_SIZE).astype(jnp.float32)
    position = jnp.arange(TOKENS_PER_LINE, dtype=jnp.int32)
    visible_mask = (position[:, None] // QLEN == position[None, :] // QLEN) & (position[None, :] <= position[:, None])
    block_list = TOKEN_TOTAL // TOKENS_PER_LINE
    context_rows = lax.map(lambda paired_blocks: block_attention(paired_blocks, document_keys, document_values, visible_mask), (queries.reshape(block_list, TOKENS_PER_LINE, QUERY_HEADS * HEAD_SIZE), question_key_values.reshape(block_list, TOKENS_PER_LINE, 2 * KEY_VALUE_HEADS * HEAD_SIZE)))
    context_rows = context_rows.reshape(TOKEN_TOTAL, QUERY_HEADS * HEAD_SIZE)
    mixture = residual_in.astype(jnp.float32) + jnp.dot(context_rows, out_proj, preferred_element_type=jnp.float32)
    normed = (mixture * lax.rsqrt(lax.optimization_barrier(jnp.mean(mixture * mixture, axis=-1, keepdims=True)) + 1e-06) * norm_gain).astype(jnp.bfloat16)
    flat_experts = jnp.where(keep_mask.reshape(-1) > 0, routes.reshape(-1), EXPERTS).astype(jnp.int32)
    order = jnp.argsort(flat_experts, stable=True).astype(jnp.int32)
    numbers = jnp.arange(EXPERTS, dtype=jnp.int32)
    counts = lax.optimization_barrier(jnp.sum((flat_experts[:, None] == numbers[None, :]).astype(jnp.int32), axis=0)).astype(jnp.int32)
    starts = (jnp.cumsum(counts) - counts).astype(jnp.int32)
    block_rows = 128
    order_padded = jnp.concatenate([order, jnp.zeros((block_rows,), jnp.int32)])
    weights_flat = route_weights.reshape(-1)
    lane_index = jnp.arange(block_rows, dtype=jnp.int32)

    def expert_step(expert, expert_total):
        slot_number = expert_slots[expert]
        gate_weights = lax.dynamic_index_in_dim(expert_gate, slot_number, 0, keepdims=False)
        up_weights = lax.dynamic_index_in_dim(expert_up, slot_number, 0, keepdims=False)
        down_weights = lax.dynamic_index_in_dim(expert_down, slot_number, 0, keepdims=False)
        load_count = counts[expert]
        load_start = starts[expert]

        def unfinished(loop_state):
            return loop_state[0] * block_rows < load_count

        def run_block(loop_state):
            block_number, running = loop_state
            pair_index = lax.dynamic_slice_in_dim(order_padded, load_start + block_number * block_rows, block_rows)
            valid = lane_index < load_count - block_number * block_rows
            token_index = (pair_index // TOPK).astype(jnp.int32)
            picked_rows = normed[token_index]
            gate_proj = jnp.dot(picked_rows, gate_weights, preferred_element_type=jnp.float32)
            upper = jnp.dot(picked_rows, up_weights, preferred_element_type=jnp.float32)
            middle = (jax.nn.silu(gate_proj) * upper).astype(jnp.bfloat16)
            answer = jnp.dot(middle, down_weights, preferred_element_type=jnp.float32).astype(jnp.bfloat16)
            answer = lax.optimization_barrier(answer).astype(jnp.float32)
            scaled = answer * jnp.where(valid, weights_flat[pair_index], 0.0)[:, None]
            return (block_number + 1, running.at[token_index].add(scaled))
        return lax.while_loop(unfinished, run_block, (jnp.int32(0), expert_total))[1]
    expert_sum = lax.fori_loop(0, EXPERTS, expert_step, jnp.zeros((TOKEN_TOTAL, D), jnp.float32))
    return (mixture + expert_sum).astype(jnp.bfloat16)
```

```python
import math

import jax
import jax.numpy as jnp
from jax import lax
from jax.sharding import PartitionSpec as P

QUERY_HEADS = 16
KEY_VALUE_HEADS = 2
HEAD_SIZE = 128
QLEN = 16


def attention(queries, local_kv, prefix):
    tokens = queries.shape[0]
    group = QUERY_HEADS // KEY_VALUE_HEADS
    scale = 1.0 / math.sqrt(HEAD_SIZE)
    width = KEY_VALUE_HEADS * HEAD_SIZE
    heads = queries.reshape(tokens, KEY_VALUE_HEADS, group, HEAD_SIZE)
    near_k = local_kv[:, :width].reshape(tokens, KEY_VALUE_HEADS, HEAD_SIZE)
    near_v = local_kv[:, width:].reshape(tokens, KEY_VALUE_HEADS, HEAD_SIZE)
    near = (
        jnp.einsum("thgd,shd->thgs", heads, near_k, preferred_element_type=jnp.float32) * scale
    )
    position = jnp.arange(tokens, dtype=jnp.int32)
    visible = (position[:, None] // QLEN == position[None, :] // QLEN) & (
        position[None, :] <= position[:, None]
    )
    near = jnp.where(visible[:, None, None, :], near, -1e30)
    top = near.max(-1)
    terms = jnp.exp(near - top[..., None])
    total = terms.sum(-1)
    acc = jnp.einsum(
        "thgs,shd->thgd", terms.astype(jnp.bfloat16), near_v, preferred_element_type=jnp.float32
    )
    rows = prefix.shape[0]
    block = math.gcd(rows, 2048)

    def step(carry, piece):
        old_max, old_sum, old_acc = carry
        keys = piece[:, :width].reshape(block, KEY_VALUE_HEADS, HEAD_SIZE)
        values = piece[:, width:].reshape(block, KEY_VALUE_HEADS, HEAD_SIZE)
        far = jnp.einsum("thgd,nhd->thgn", heads, keys, preferred_element_type=jnp.float32) * scale
        new_max = jnp.maximum(old_max, far.max(-1))
        factor = jnp.exp(old_max - new_max)
        far = jnp.exp(far - new_max[..., None])
        new_acc = old_acc * factor[..., None] + jnp.einsum(
            "thgn,nhd->thgd", far.astype(jnp.bfloat16), values, preferred_element_type=jnp.float32
        )
        return (new_max, old_sum * factor + far.sum(-1), new_acc), None

    (top, total, acc), _ = lax.scan(
        step, (top, total, acc), prefix.reshape(rows // block, block, 2 * width)
    )
    return (acc / total[..., None]).reshape(tokens, QUERY_HEADS * HEAD_SIZE).astype(jnp.bfloat16)


def body(
    residual_in,
    queries,
    question_key_values,
    document_prefix_cache,
    out_proj,
    norm_gain,
    routes,
    keep_mask,
    route_weights,
    expert_slots,
    expert_gate,
    expert_up,
    expert_down,
):
    prefix = lax.all_gather(document_prefix_cache, "line", axis=0, tiled=True)
    projection = lax.all_gather(out_proj, "line", axis=0, tiled=True)
    numbers = jnp.arange(expert_slots.shape[0], dtype=jnp.int32)
    slot_of_number = expert_slots[None, :] == numbers[:, None]
    number_of_slot = jnp.sum(jnp.where(slot_of_number, numbers[None, :], 0), axis=1)
    kept = jnp.where(keep_mask > 0, route_weights, 0.0)
    per_slot = jnp.sum(
        jnp.where(routes[:, :, None] == number_of_slot[None, None, :], kept[:, :, None], 0.0),
        axis=1,
    )
    all_slots = lax.all_gather(per_slot, "line", axis=0, tiled=True)
    weight = lax.dynamic_slice_in_dim(all_slots, lax.axis_index("line"), 1, 1)
    context = attention(queries, question_key_values, prefix)
    attended = jnp.dot(context, projection, preferred_element_type=jnp.float32)
    mixture = residual_in.astype(jnp.float32) + attended
    normed = (
        mixture * lax.rsqrt(jnp.mean(mixture * mixture, axis=-1, keepdims=True) + 1e-06) * norm_gain
    ).astype(jnp.bfloat16)
    rows = lax.all_gather(normed, "line", axis=0, tiled=True)
    gate = jnp.dot(rows, expert_gate[0], preferred_element_type=jnp.float32)
    upper = jnp.dot(rows, expert_up[0], preferred_element_type=jnp.float32)
    middle = (jax.nn.silu(gate) * upper).astype(jnp.bfloat16)
    answer = jnp.dot(middle, expert_down[0], preferred_element_type=jnp.float32)
    share = (answer.astype(jnp.bfloat16).astype(jnp.float32) * weight).astype(jnp.bfloat16)
    summed = lax.psum_scatter(share, "line", scatter_dimension=0, tiled=True)
    return (mixture + summed.astype(jnp.float32)).astype(jnp.bfloat16)


def solution(mesh):
    rows = P(("group", "line"), None)
    expert = P("line", None, None)
    placed = (rows, rows, rows, rows, P("line", None), P(), rows, rows, rows, P())
    return jax.shard_map(
        body,
        mesh=mesh,
        in_specs=placed + (expert, expert, expert),
        out_specs=rows,
        check_vma=False,
    )
```

```python
import functools
import math

import jax
import jax.numpy as jnp
from jax import lax
from jax.experimental import pallas as pl
from jax.experimental.pallas import tpu as pltpu
from jax.sharding import PartitionSpec as P

QUERY_HEADS = 16
KEY_VALUE_HEADS = 2
HEAD_SIZE = 128
QLEN = 16


MESH = pl.DeviceIdType.MESH
PLANE = 4


def place(levels):
    line = lax.axis_index("line")
    group = lax.axis_index("group")
    level, side, core = line // PLANE, (line // 2) % 2, line % 2

    def device(level, side, core):
        return (group, level * PLANE + side * 2 + core)

    barrier = pltpu.get_barrier_semaphore()
    has_up, has_down = level + 1 < levels, level > 0

    def greet(target):
        pl.semaphore_signal(barrier, inc=1, device_id=target, device_id_type=MESH)

    greet(device(level, 1 - side, core))
    greet(device(level, side, 1 - core))
    pl.when(has_up)(lambda: greet(device(level + 1, side, core)))
    pl.when(has_down)(lambda: greet(device(level - 1, side, core)))
    inner = has_up & has_down
    pl.when(inner)(lambda: pl.semaphore_wait(barrier, 4))
    pl.when(jnp.logical_not(inner))(lambda: pl.semaphore_wait(barrier, 3))
    return level, side, core, device, has_up, has_down


def run_if(condition, action):
    if condition is None:
        action()
    else:
        pl.when(condition)(action)


def both(first, second):
    return second if first is None else first & second


def gather_kernel(levels, arrays, *refs):
    ins, outs = refs[:arrays], refs[arrays : 2 * arrays]
    up_sem, down_sem, side_sem, core_sem, recv_sem, own_sem = refs[2 * arrays :]
    level, side, core, device, has_up, has_down = place(levels)
    above, below = device(level + 1, side, core), device(level - 1, side, core)
    across, twin = device(level, 1 - side, core), device(level, side, 1 - core)
    pending = []

    def slot_of(at_level, at_side, at_core):
        return at_level * PLANE + at_side * 2 + at_core

    def send(array, slot, source, target, sem, condition):
        copy = pltpu.make_async_remote_copy(
            src_ref=source,
            dst_ref=outs[array].at[slot],
            send_sem=sem,
            recv_sem=recv_sem.at[array, slot],
            device_id=target,
            device_id_type=MESH,
        )
        run_if(condition, copy.start)
        pending.append((condition, copy))

    def arrived(array, slot, condition):
        copy = pltpu.make_async_remote_copy(
            src_ref=outs[array].at[slot],
            dst_ref=outs[array].at[slot],
            send_sem=own_sem.at[array],
            recv_sem=recv_sem.at[array, slot],
            device_id=twin,
            device_id_type=MESH,
        )
        run_if(condition, copy.wait_recv)

    mine = slot_of(level, side, core)
    own = []
    for array in range(arrays):
        source = ins[array]
        send(array, mine, source, above, up_sem.at[array, 0], has_up)
        send(array, mine, source, below, down_sem.at[array, 0], has_down)
        send(array, mine, source, across, side_sem.at[array, 0], None)
        send(array, mine, source, twin, core_sem.at[array, 0], None)
        copy = pltpu.make_async_copy(source, outs[array].at[mine], own_sem.at[array])
        copy.start()
        own.append(copy)
    for hop in range(1, levels):
        for array in range(arrays):
            there = level - hop >= 0
            slot = slot_of(level - hop, side, core)
            source = outs[array].at[slot]
            arrived(array, slot, there)
            send(array, slot, source, above, up_sem.at[array, hop], there & has_up)
            send(array, slot, source, across, side_sem.at[array, 2 * hop - 1], there)
            send(array, slot, source, twin, core_sem.at[array, 2 * hop - 1], there)
            there = level + hop < levels
            slot = slot_of(level + hop, side, core)
            source = outs[array].at[slot]
            arrived(array, slot, there)
            send(array, slot, source, below, down_sem.at[array, hop], there & has_down)
            send(array, slot, source, across, side_sem.at[array, 2 * hop], there)
            send(array, slot, source, twin, core_sem.at[array, 2 * hop], there)
    base = 2 * levels
    for hop in range(levels):
        for array in range(arrays):
            for sign in (-1, 1) if hop else (1,):
                at_level = level + sign * hop
                there = (at_level >= 0) & (at_level < levels) if hop else None
                slot = slot_of(at_level, 1 - side, core)
                arrived(array, slot, there)
                index = base + 2 * hop + (sign + 1) // 2
                send(array, slot, outs[array].at[slot], twin, core_sem.at[array, index], there)
    for array in range(arrays):
        for at_level in range(levels):
            for at_side in range(2):
                arrived(array, slot_of(at_level, at_side, 1 - core), None)
        own[array].wait()
    for condition, copy in pending:
        run_if(condition, copy.wait_send)


def gather(levels, identity, *arrays):
    count = len(arrays)
    devices = levels * PLANE
    sem = pltpu.SemaphoreType.DMA
    anywhere = pl.BlockSpec(memory_space=pl.ANY)
    outs = pl.pallas_call(
        functools.partial(gather_kernel, levels, count),
        out_shape=[jax.ShapeDtypeStruct((devices,) + a.shape, a.dtype) for a in arrays],
        in_specs=[anywhere] * count,
        out_specs=[anywhere] * count,
        scratch_shapes=[
            sem((count, levels)),
            sem((count, levels)),
            sem((count, 2 * levels)),
            sem((count, 4 * levels)),
            sem((count, devices)),
            sem((count,)),
        ],
        compiler_params=pltpu.CompilerParams(collective_id=identity, has_side_effects=True),
    )(*arrays)
    return [out.reshape((-1, out.shape[-1])) for out in outs]


def scatter_kernel(
    levels,
    share,
    out,
    core_in,
    side_in,
    up_in,
    down_in,
    side_out,
    z_out,
    core_send,
    core_recv,
    side_send,
    side_recv,
    z_send,
    up_recv,
    down_recv,
):
    level, side, core, device, has_up, has_down = place(levels)
    above, below = device(level + 1, side, core), device(level - 1, side, core)
    across, twin = device(level, 1 - side, core), device(level, side, 1 - core)
    wide = jnp.float32

    def copy(source, landing, sem, recv, target):
        return pltpu.make_async_remote_copy(
            src_ref=source,
            dst_ref=landing,
            send_sem=sem,
            recv_sem=recv,
            device_id=target,
            device_id_type=MESH,
        )

    order = []
    for step in range(levels // 2):
        order += [levels - 1 - step, step]
    pending = []
    core_copies = {}
    for far in (1, 0):
        for at in order:
            at_side = 1 - side if far else side
            block = share.at[at * PLANE + at_side * 2 + (1 - core)]
            index = at * 2 + far
            one = copy(
                block, core_in.at[index], core_send.at[index], core_recv.at[index], twin
            )
            one.start()
            pending.append((None, one))
            core_copies[index] = one
    side_copies = {}
    for at in order:
        core_copies[at * 2 + 1].wait_recv()
        slot = at * PLANE + (1 - side) * 2 + core
        side_out[at] = (share[slot].astype(wide) + core_in[at * 2 + 1].astype(wide)).astype(
            side_out.dtype
        )
        one = copy(side_out.at[at], side_in.at[at], side_send.at[at], side_recv.at[at], across)
        one.start()
        pending.append((None, one))
        side_copies[at] = one
    for at in order:
        core_copies[at * 2].wait_recv()
        side_copies[at].wait_recv()
        up = copy(z_out.at[at], up_in.at[at], z_send.at[at], up_recv.at[at], above)
        down = copy(z_out.at[at], down_in.at[at], z_send.at[at], down_recv.at[at], below)

        def local(at=at):
            slot = at * PLANE + side * 2 + core
            return (
                share[slot].astype(wide)
                + core_in[at * 2].astype(wide)
                + side_in[at].astype(wide)
            )

        def start(value, one, at=at):
            z_out[at] = value.astype(z_out.dtype)
            one.start()

        def climb(at=at, up=up, local=local, start=start):
            up.wait_recv()
            start(local() + up_in[at].astype(wide), up)

        def drop(at=at, down=down, local=local, start=start):
            down.wait_recv()
            start(local() + down_in[at].astype(wide), down)

        def keep(local=local):
            out[...] = local()

        pl.when((at > level) & has_down)(climb)
        pl.when((at > level) & (level == 0))(lambda: start(local(), up))
        pl.when((at < level) & has_up)(drop)
        pl.when((at < level) & (level == levels - 1))(lambda: start(local(), down))
        pl.when(at == level)(keep)
        pending.append((at > level, up))
        pending.append((at < level, down))

    for at in range(levels):
        up = copy(z_out.at[at], up_in.at[at], z_send.at[at], up_recv.at[at], above)
        down = copy(z_out.at[at], down_in.at[at], z_send.at[at], down_recv.at[at], below)

        def take_up(at=at, up=up):
            up.wait_recv()
            out[...] += up_in[at].astype(wide)

        def take_down(at=at, down=down):
            down.wait_recv()
            out[...] += down_in[at].astype(wide)

        pl.when((at == level) & has_down)(take_up)
        pl.when((at == level) & has_up)(take_down)
    for condition, one in pending:
        run_if(condition, one.wait_send)


def scatter(levels, identity, share):
    devices = levels * PLANE
    rows, width = share.shape[0] // devices, share.shape[1]
    sem = pltpu.SemaphoreType.DMA
    block = (rows, width)
    vmem = pl.BlockSpec(memory_space=pltpu.VMEM)
    return pl.pallas_call(
        functools.partial(scatter_kernel, levels),
        out_shape=jax.ShapeDtypeStruct(block, jnp.float32),
        in_specs=[vmem],
        out_specs=vmem,
        scratch_shapes=[
            pltpu.VMEM((2 * levels,) + block, share.dtype),
            pltpu.VMEM((levels,) + block, share.dtype),
            pltpu.VMEM((levels,) + block, share.dtype),
            pltpu.VMEM((levels,) + block, share.dtype),
            pltpu.VMEM((levels,) + block, share.dtype),
            pltpu.VMEM((levels,) + block, share.dtype),
            sem((2 * levels,)),
            sem((2 * levels,)),
            sem((levels,)),
            sem((levels,)),
            sem((levels,)),
            sem((levels,)),
            sem((levels,)),
        ],
        compiler_params=pltpu.CompilerParams(
            collective_id=identity, has_side_effects=True, vmem_limit_bytes=40 * 1024 * 1024
        ),
    )(share.reshape((devices,) + block))


def attention(queries, local_kv, prefix):
    tokens = queries.shape[0]
    group = QUERY_HEADS // KEY_VALUE_HEADS
    scale = 1.0 / math.sqrt(HEAD_SIZE)
    width = KEY_VALUE_HEADS * HEAD_SIZE
    heads = queries.reshape(tokens, KEY_VALUE_HEADS, group, HEAD_SIZE)
    near_k = local_kv[:, :width].reshape(tokens, KEY_VALUE_HEADS, HEAD_SIZE)
    near_v = local_kv[:, width:].reshape(tokens, KEY_VALUE_HEADS, HEAD_SIZE)
    near = (
        jnp.einsum("thgd,shd->thgs", heads, near_k, preferred_element_type=jnp.float32) * scale
    )
    position = jnp.arange(tokens, dtype=jnp.int32)
    visible = (position[:, None] // QLEN == position[None, :] // QLEN) & (
        position[None, :] <= position[:, None]
    )
    near = jnp.where(visible[:, None, None, :], near, -1e30)
    top = near.max(-1)
    terms = jnp.exp(near - top[..., None])
    total = terms.sum(-1)
    acc = jnp.einsum(
        "thgs,shd->thgd", terms.astype(jnp.bfloat16), near_v, preferred_element_type=jnp.float32
    )
    rows = prefix.shape[0]
    block = math.gcd(rows, 2048)

    def step(carry, piece):
        old_max, old_sum, old_acc = carry
        keys = piece[:, :width].reshape(block, KEY_VALUE_HEADS, HEAD_SIZE)
        values = piece[:, width:].reshape(block, KEY_VALUE_HEADS, HEAD_SIZE)
        far = jnp.einsum("thgd,nhd->thgn", heads, keys, preferred_element_type=jnp.float32) * scale
        new_max = jnp.maximum(old_max, far.max(-1))
        factor = jnp.exp(old_max - new_max)
        far = jnp.exp(far - new_max[..., None])
        new_acc = old_acc * factor[..., None] + jnp.einsum(
            "thgn,nhd->thgd", far.astype(jnp.bfloat16), values, preferred_element_type=jnp.float32
        )
        return (new_max, old_sum * factor + far.sum(-1), new_acc), None

    (top, total, acc), _ = lax.scan(
        step, (top, total, acc), prefix.reshape(rows // block, block, 2 * width)
    )
    return (acc / total[..., None]).reshape(tokens, QUERY_HEADS * HEAD_SIZE).astype(jnp.bfloat16)


def body(
    residual_in,
    queries,
    question_key_values,
    document_prefix_cache,
    out_proj,
    norm_gain,
    routes,
    keep_mask,
    route_weights,
    expert_slots,
    expert_gate,
    expert_up,
    expert_down,
):
    count = lax.axis_size("line")
    small = count % (2 * PLANE) == 0 and count * queries.shape[0] <= 2048
    levels = count // PLANE
    numbers = jnp.arange(expert_slots.shape[0], dtype=jnp.int32)
    slot_of_number = expert_slots[None, :] == numbers[:, None]
    number_of_slot = jnp.sum(jnp.where(slot_of_number, numbers[None, :], 0), axis=1)
    kept = jnp.where(keep_mask > 0, route_weights, 0.0)
    per_slot = jnp.sum(
        jnp.where(routes[:, :, None] == number_of_slot[None, None, :], kept[:, :, None], 0.0),
        axis=1,
    )
    if small:
        per_slot = jnp.pad(per_slot, ((0, 0), (0, -per_slot.shape[1] % 128)))
        prefix, projection, all_slots = gather(
            levels, 0, document_prefix_cache, out_proj, per_slot
        )
    else:
        prefix = lax.all_gather(document_prefix_cache, "line", axis=0, tiled=True)
        projection = lax.all_gather(out_proj, "line", axis=0, tiled=True)
        all_slots = lax.all_gather(per_slot, "line", axis=0, tiled=True)
    weight = lax.dynamic_slice_in_dim(all_slots, lax.axis_index("line"), 1, 1)
    context = attention(queries, question_key_values, prefix)
    attended = jnp.dot(context, projection, preferred_element_type=jnp.float32)
    mixture = residual_in.astype(jnp.float32) + attended
    normed = (
        mixture * lax.rsqrt(jnp.mean(mixture * mixture, axis=-1, keepdims=True) + 1e-06) * norm_gain
    ).astype(jnp.bfloat16)
    if small:
        (rows,) = gather(levels, 1, normed)
    else:
        rows = lax.all_gather(normed, "line", axis=0, tiled=True)
    gate = jnp.dot(rows, expert_gate[0], preferred_element_type=jnp.float32)
    upper = jnp.dot(rows, expert_up[0], preferred_element_type=jnp.float32)
    middle = (jax.nn.silu(gate) * upper).astype(jnp.bfloat16)
    answer = jnp.dot(middle, expert_down[0], preferred_element_type=jnp.float32)
    share = (answer.astype(jnp.bfloat16).astype(jnp.float32) * weight).astype(jnp.bfloat16)
    if small:
        summed = scatter(levels, 2, share)
    else:
        summed = lax.psum_scatter(share, "line", scatter_dimension=0, tiled=True)
    return (mixture + summed.astype(jnp.float32)).astype(jnp.bfloat16)


def solution(mesh):
    rows = P(("group", "line"), None)
    expert = P("line", None, None)
    placed = (rows, rows, rows, rows, P("line", None), P(), rows, rows, rows, P())
    return jax.shard_map(
        body,
        mesh=mesh,
        in_specs=placed + (expert, expert, expert),
        out_specs=rows,
        check_vma=False,
    )
```

```python
import functools
import math

import jax
import jax.numpy as jnp
from jax import lax
from jax.experimental import pallas as pl
from jax.experimental.pallas import tpu as pltpu
from jax.sharding import PartitionSpec as P

QUERY_HEADS = 16
KEY_VALUE_HEADS = 2
HEAD_SIZE = 128
QLEN = 16


MESH = pl.DeviceIdType.MESH
PLANE = 4


def place(levels, pair=False):
    line = lax.axis_index("line")
    group = lax.axis_index("group")
    level, side, core = line // PLANE, (line // 2) % 2, line % 2

    def device(level, side, core):
        return (group, level * PLANE + side * 2 + core)

    barrier = pltpu.get_barrier_semaphore()
    has_up, has_down = level + 1 < levels, level > 0

    def greet(target):
        pl.semaphore_signal(barrier, inc=1, device_id=target, device_id_type=MESH)

    if pair:
        greet((1 - group, line))
    extra = 1 if pair else 0
    greet(device(level, 1 - side, core))
    greet(device(level, side, 1 - core))
    pl.when(has_up)(lambda: greet(device(level + 1, side, core)))
    pl.when(has_down)(lambda: greet(device(level - 1, side, core)))
    inner = has_up & has_down
    pl.when(inner)(lambda: pl.semaphore_wait(barrier, 4 + extra))
    pl.when(jnp.logical_not(inner))(lambda: pl.semaphore_wait(barrier, 3 + extra))
    return level, side, core, device, has_up, has_down


def run_if(condition, action):
    if condition is None:
        action()
    else:
        pl.when(condition)(action)


def both(first, second):
    return second if first is None else first & second


def gather_kernel(levels, arrays, shared, *refs):
    ins, outs = refs[:arrays], refs[arrays : 2 * arrays]
    up_sem, down_sem, side_sem, core_sem, recv_sem, own_sem = refs[2 * arrays : 2 * arrays + 6]
    pair_send, pair_core, pair_recv = refs[2 * arrays + 6 :]
    level, side, core, device, has_up, has_down = place(levels, shared is not None)
    group = lax.axis_index("group")
    peer = (1 - group, lax.axis_index("line"))
    above, below = device(level + 1, side, core), device(level - 1, side, core)
    across, twin = device(level, 1 - side, core), device(level, side, 1 - core)
    pending = []

    def slot_of(at_level, at_side, at_core):
        return at_level * PLANE + at_side * 2 + at_core

    def part_of(array, ref, which):
        if which is None:
            return ref
        half = ins[array].shape[0] // 2
        return ref.at[pl.ds(pl.multiple_of(which * half, half), half)]

    def send(array, slot, source, target, sem, condition, which=None, recv=None):
        copy = pltpu.make_async_remote_copy(
            src_ref=part_of(array, source, which),
            dst_ref=part_of(array, outs[array].at[slot], which),
            send_sem=sem,
            recv_sem=recv_sem.at[array, slot] if recv is None else recv,
            device_id=target,
            device_id_type=MESH,
        )
        run_if(condition, copy.start)
        pending.append((condition, copy))

    def half_of(array):
        return group if array == shared else None

    def arrived(array, slot, condition, which=None, recv=None):
        landing = part_of(array, outs[array].at[slot], which)
        copy = pltpu.make_async_remote_copy(
            src_ref=landing,
            dst_ref=landing,
            send_sem=own_sem.at[array],
            recv_sem=recv_sem.at[array, slot] if recv is None else recv,
            device_id=twin,
            device_id_type=MESH,
        )
        run_if(condition, copy.wait_recv)

    mine = slot_of(level, side, core)
    own = []
    for array in range(arrays):
        source = ins[array]
        send(array, mine, source, above, up_sem.at[array, 0], has_up)
        send(array, mine, source, below, down_sem.at[array, 0], has_down)
        send(array, mine, source, across, side_sem.at[array, 0], None, half_of(array))
        send(array, mine, source, twin, core_sem.at[array, 0], None)
        copy = pltpu.make_async_copy(source, outs[array].at[mine], own_sem.at[array])
        copy.start()
        own.append(copy)
    for hop in range(1, levels):
        for array in range(arrays):
            there = level - hop >= 0
            slot = slot_of(level - hop, side, core)
            source = outs[array].at[slot]
            arrived(array, slot, there)
            send(array, slot, source, above, up_sem.at[array, hop], there & has_up)
            send(array, slot, source, across, side_sem.at[array, 2 * hop - 1], there, half_of(array))
            send(array, slot, source, twin, core_sem.at[array, 2 * hop - 1], there)
            there = level + hop < levels
            slot = slot_of(level + hop, side, core)
            source = outs[array].at[slot]
            arrived(array, slot, there)
            send(array, slot, source, below, down_sem.at[array, hop], there & has_down)
            send(array, slot, source, across, side_sem.at[array, 2 * hop], there, half_of(array))
            send(array, slot, source, twin, core_sem.at[array, 2 * hop], there)
    base = 2 * levels
    for stage in range(2):
        for hop in range(levels):
            for array in range(arrays):
                if stage == 1 and array != shared:
                    continue
                for sign in (-1, 1) if hop else (1,):
                    at_level = level + sign * hop
                    there = (at_level >= 0) & (at_level < levels) if hop else None
                    slot = slot_of(at_level, 1 - side, core)
                    index = 2 * hop + (sign + 1) // 2
                    source = outs[array].at[slot]
                    if stage == 0:
                        half = half_of(array)
                        arrived(array, slot, there, half)
                        if array == shared:
                            send(
                                array,
                                slot,
                                source,
                                peer,
                                pair_send.at[index],
                                there,
                                half,
                                pair_recv.at[slot],
                            )
                        sem = core_sem.at[array, base + index]
                        send(array, slot, source, twin, sem, there, half)
                    else:
                        half = 1 - group
                        arrived(array, slot, there, half, pair_recv.at[slot])
                        sem = pair_core.at[index]
                        send(array, slot, source, twin, sem, there, half, pair_recv.at[slot])
    for array in range(arrays):
        for at_level in range(levels):
            arrived(array, slot_of(at_level, side, 1 - core), None)
            slot = slot_of(at_level, 1 - side, 1 - core)
            arrived(array, slot, None, half_of(array))
            if array == shared:
                arrived(array, slot, None, 1 - group, pair_recv.at[slot])
        own[array].wait()
    for condition, copy in pending:
        run_if(condition, copy.wait_send)


def gather(levels, identity, *arrays, shared=None):
    count = len(arrays)
    devices = levels * PLANE
    sem = pltpu.SemaphoreType.DMA
    anywhere = pl.BlockSpec(memory_space=pl.ANY)
    outs = pl.pallas_call(
        functools.partial(gather_kernel, levels, count, shared),
        out_shape=[jax.ShapeDtypeStruct((devices,) + a.shape, a.dtype) for a in arrays],
        in_specs=[anywhere] * count,
        out_specs=[anywhere] * count,
        scratch_shapes=[
            sem((count, levels)),
            sem((count, levels)),
            sem((count, 2 * levels)),
            sem((count, 4 * levels)),
            sem((count, devices)),
            sem((count,)),
            sem((2 * levels,)),
            sem((2 * levels,)),
            sem((devices,)),
        ],
        compiler_params=pltpu.CompilerParams(collective_id=identity, has_side_effects=True),
    )(*arrays)
    return [out.reshape((-1, out.shape[-1])) for out in outs]


def scatter_kernel(
    levels,
    share,
    out,
    core_in,
    side_in,
    up_in,
    down_in,
    side_out,
    z_out,
    core_send,
    core_recv,
    side_send,
    side_recv,
    z_send,
    up_recv,
    down_recv,
):
    level, side, core, device, has_up, has_down = place(levels)
    above, below = device(level + 1, side, core), device(level - 1, side, core)
    across, twin = device(level, 1 - side, core), device(level, side, 1 - core)
    wide = jnp.float32

    def copy(source, landing, sem, recv, target):
        return pltpu.make_async_remote_copy(
            src_ref=source,
            dst_ref=landing,
            send_sem=sem,
            recv_sem=recv,
            device_id=target,
            device_id_type=MESH,
        )

    order = []
    for step in range(levels // 2):
        order += [levels - 1 - step, step]
    pending = []
    core_copies = {}
    for far in (1, 0):
        for at in order:
            at_side = 1 - side if far else side
            block = share.at[at * PLANE + at_side * 2 + (1 - core)]
            index = at * 2 + far
            one = copy(
                block, core_in.at[index], core_send.at[index], core_recv.at[index], twin
            )
            one.start()
            pending.append((None, one))
            core_copies[index] = one
    side_copies = {}
    for at in order:
        core_copies[at * 2 + 1].wait_recv()
        slot = at * PLANE + (1 - side) * 2 + core
        side_out[at] = (share[slot].astype(wide) + core_in[at * 2 + 1].astype(wide)).astype(
            side_out.dtype
        )
        one = copy(side_out.at[at], side_in.at[at], side_send.at[at], side_recv.at[at], across)
        one.start()
        pending.append((None, one))
        side_copies[at] = one
    for at in order:
        core_copies[at * 2].wait_recv()
        side_copies[at].wait_recv()
        up = copy(z_out.at[at], up_in.at[at], z_send.at[at], up_recv.at[at], above)
        down = copy(z_out.at[at], down_in.at[at], z_send.at[at], down_recv.at[at], below)

        def local(at=at):
            slot = at * PLANE + side * 2 + core
            return (
                share[slot].astype(wide)
                + core_in[at * 2].astype(wide)
                + side_in[at].astype(wide)
            )

        def start(value, one, at=at):
            z_out[at] = value.astype(z_out.dtype)
            one.start()

        def climb(at=at, up=up, local=local, start=start):
            up.wait_recv()
            start(local() + up_in[at].astype(wide), up)

        def drop(at=at, down=down, local=local, start=start):
            down.wait_recv()
            start(local() + down_in[at].astype(wide), down)

        def keep(local=local):
            out[...] = local()

        pl.when((at > level) & has_down)(climb)
        pl.when((at > level) & (level == 0))(lambda: start(local(), up))
        pl.when((at < level) & has_up)(drop)
        pl.when((at < level) & (level == levels - 1))(lambda: start(local(), down))
        pl.when(at == level)(keep)
        pending.append((at > level, up))
        pending.append((at < level, down))

    for at in range(levels):
        up = copy(z_out.at[at], up_in.at[at], z_send.at[at], up_recv.at[at], above)
        down = copy(z_out.at[at], down_in.at[at], z_send.at[at], down_recv.at[at], below)

        def take_up(at=at, up=up):
            up.wait_recv()
            out[...] += up_in[at].astype(wide)

        def take_down(at=at, down=down):
            down.wait_recv()
            out[...] += down_in[at].astype(wide)

        pl.when((at == level) & has_down)(take_up)
        pl.when((at == level) & has_up)(take_down)
    for condition, one in pending:
        run_if(condition, one.wait_send)


def scatter(levels, identity, share):
    devices = levels * PLANE
    rows, width = share.shape[0] // devices, share.shape[1]
    sem = pltpu.SemaphoreType.DMA
    block = (rows, width)
    vmem = pl.BlockSpec(memory_space=pltpu.VMEM)
    return pl.pallas_call(
        functools.partial(scatter_kernel, levels),
        out_shape=jax.ShapeDtypeStruct(block, jnp.float32),
        in_specs=[vmem],
        out_specs=vmem,
        scratch_shapes=[
            pltpu.VMEM((2 * levels,) + block, share.dtype),
            pltpu.VMEM((levels,) + block, share.dtype),
            pltpu.VMEM((levels,) + block, share.dtype),
            pltpu.VMEM((levels,) + block, share.dtype),
            pltpu.VMEM((levels,) + block, share.dtype),
            pltpu.VMEM((levels,) + block, share.dtype),
            sem((2 * levels,)),
            sem((2 * levels,)),
            sem((levels,)),
            sem((levels,)),
            sem((levels,)),
            sem((levels,)),
            sem((levels,)),
        ],
        compiler_params=pltpu.CompilerParams(
            collective_id=identity, has_side_effects=True, vmem_limit_bytes=40 * 1024 * 1024
        ),
    )(share.reshape((devices,) + block))


def attend_kernel(q_ref, key_ref, value_ref, near_key_ref, near_value_ref, out_ref):
    tokens = q_ref.shape[0]
    heads = q_ref.shape[1] // HEAD_SIZE
    scale = 1.0 / math.sqrt(HEAD_SIZE)
    q = jnp.concatenate(
        [q_ref[:, i * HEAD_SIZE : (i + 1) * HEAD_SIZE] for i in range(heads)], axis=0
    )
    dims = (((1,), (1,)), ((), ()))
    far = lax.dot_general(q, key_ref[...], dims, preferred_element_type=jnp.float32) * scale
    near = lax.dot_general(q, near_key_ref[...], dims, preferred_element_type=jnp.float32) * scale
    token = lax.rem(lax.broadcasted_iota(jnp.int32, near.shape, 0), tokens)
    other = lax.broadcasted_iota(jnp.int32, near.shape, 1)
    near = jnp.where((token // QLEN == other // QLEN) & (other <= token), near, -1e30)
    top = jnp.maximum(far.max(-1, keepdims=True), near.max(-1, keepdims=True))
    far = jnp.exp(far - top)
    near = jnp.exp(near - top)
    total = far.sum(-1, keepdims=True) + near.sum(-1, keepdims=True)
    acc = jnp.dot(far.astype(jnp.bfloat16), value_ref[...], preferred_element_type=jnp.float32)
    acc += jnp.dot(
        near.astype(jnp.bfloat16), near_value_ref[...], preferred_element_type=jnp.float32
    )
    context = (acc / total).astype(out_ref.dtype)
    for i in range(heads):
        out_ref[:, i * HEAD_SIZE : (i + 1) * HEAD_SIZE] = context[i * tokens : (i + 1) * tokens]


def attend(queries, local_kv, prefix):
    tokens, rows = queries.shape[0], prefix.shape[0]
    wide = 4 * HEAD_SIZE
    steps = QUERY_HEADS // KEY_VALUE_HEADS // 4
    return pl.pallas_call(
        attend_kernel,
        grid=(KEY_VALUE_HEADS, steps),
        out_shape=jax.ShapeDtypeStruct(queries.shape, queries.dtype),
        in_specs=[
            pl.BlockSpec((tokens, wide), lambda g, i: (0, g * steps + i)),
            pl.BlockSpec((rows, HEAD_SIZE), lambda g, i: (0, g)),
            pl.BlockSpec((rows, HEAD_SIZE), lambda g, i: (0, KEY_VALUE_HEADS + g)),
            pl.BlockSpec((tokens, HEAD_SIZE), lambda g, i: (0, g)),
            pl.BlockSpec((tokens, HEAD_SIZE), lambda g, i: (0, KEY_VALUE_HEADS + g)),
        ],
        out_specs=pl.BlockSpec((tokens, wide), lambda g, i: (0, g * steps + i)),
        compiler_params=pltpu.CompilerParams(vmem_limit_bytes=40 * 1024 * 1024),
    )(queries, prefix, prefix, local_kv, local_kv)


def expert_kernel(row_ref, weight_ref, gate_ref, up_ref, down_ref, out_ref):
    rows = row_ref[...]
    gate = jnp.dot(rows, gate_ref[0], preferred_element_type=jnp.float32)
    upper = jnp.dot(rows, up_ref[0], preferred_element_type=jnp.float32)
    middle = (gate / (1.0 + jnp.exp(-gate)) * upper).astype(jnp.bfloat16)
    answer = jnp.dot(middle, down_ref[0], preferred_element_type=jnp.float32)
    answer = answer.astype(jnp.bfloat16).astype(jnp.float32)
    out_ref[...] = (answer * weight_ref[...]).astype(out_ref.dtype)


def run_expert(rows, weight, gate, up, down):
    count, width = rows.shape
    block = math.gcd(count, 256)
    row_spec = pl.BlockSpec((block, width), lambda i: (i, 0))
    return pl.pallas_call(
        expert_kernel,
        grid=(count // block,),
        out_shape=jax.ShapeDtypeStruct(rows.shape, rows.dtype),
        in_specs=[
            row_spec,
            pl.BlockSpec((block, 1), lambda i: (i, 0)),
            pl.BlockSpec(gate.shape, lambda i: (0, 0, 0)),
            pl.BlockSpec(up.shape, lambda i: (0, 0, 0)),
            pl.BlockSpec(down.shape, lambda i: (0, 0, 0)),
        ],
        out_specs=row_spec,
        compiler_params=pltpu.CompilerParams(vmem_limit_bytes=48 * 1024 * 1024),
    )(rows, weight, gate, up, down)


def attention(queries, local_kv, prefix):
    tokens = queries.shape[0]
    group = QUERY_HEADS // KEY_VALUE_HEADS
    scale = 1.0 / math.sqrt(HEAD_SIZE)
    width = KEY_VALUE_HEADS * HEAD_SIZE
    heads = queries.reshape(tokens, KEY_VALUE_HEADS, group, HEAD_SIZE)
    near_k = local_kv[:, :width].reshape(tokens, KEY_VALUE_HEADS, HEAD_SIZE)
    near_v = local_kv[:, width:].reshape(tokens, KEY_VALUE_HEADS, HEAD_SIZE)
    near = (
        jnp.einsum("thgd,shd->thgs", heads, near_k, preferred_element_type=jnp.float32) * scale
    )
    position = jnp.arange(tokens, dtype=jnp.int32)
    visible = (position[:, None] // QLEN == position[None, :] // QLEN) & (
        position[None, :] <= position[:, None]
    )
    near = jnp.where(visible[:, None, None, :], near, -1e30)
    top = near.max(-1)
    terms = jnp.exp(near - top[..., None])
    total = terms.sum(-1)
    acc = jnp.einsum(
        "thgs,shd->thgd", terms.astype(jnp.bfloat16), near_v, preferred_element_type=jnp.float32
    )
    rows = prefix.shape[0]
    block = math.gcd(rows, 2048)

    def step(carry, piece):
        old_max, old_sum, old_acc = carry
        keys = piece[:, :width].reshape(block, KEY_VALUE_HEADS, HEAD_SIZE)
        values = piece[:, width:].reshape(block, KEY_VALUE_HEADS, HEAD_SIZE)
        far = jnp.einsum("thgd,nhd->thgn", heads, keys, preferred_element_type=jnp.float32) * scale
        new_max = jnp.maximum(old_max, far.max(-1))
        factor = jnp.exp(old_max - new_max)
        far = jnp.exp(far - new_max[..., None])
        new_acc = old_acc * factor[..., None] + jnp.einsum(
            "thgn,nhd->thgd", far.astype(jnp.bfloat16), values, preferred_element_type=jnp.float32
        )
        return (new_max, old_sum * factor + far.sum(-1), new_acc), None

    (top, total, acc), _ = lax.scan(
        step, (top, total, acc), prefix.reshape(rows // block, block, 2 * width)
    )
    return (acc / total[..., None]).reshape(tokens, QUERY_HEADS * HEAD_SIZE).astype(jnp.bfloat16)


def body(
    residual_in,
    queries,
    question_key_values,
    document_prefix_cache,
    out_proj,
    norm_gain,
    routes,
    keep_mask,
    route_weights,
    expert_slots,
    expert_gate,
    expert_up,
    expert_down,
):
    count = lax.axis_size("line")
    small = count % (2 * PLANE) == 0 and count * queries.shape[0] <= 2048
    levels = count // PLANE
    numbers = jnp.arange(expert_slots.shape[0], dtype=jnp.int32)
    slot_of_number = expert_slots[None, :] == numbers[:, None]
    number_of_slot = jnp.sum(jnp.where(slot_of_number, numbers[None, :], 0), axis=1)
    kept = jnp.where(keep_mask > 0, route_weights, 0.0)
    per_slot = jnp.sum(
        jnp.where(routes[:, :, None] == number_of_slot[None, None, :], kept[:, :, None], 0.0),
        axis=1,
    )
    if small:
        per_slot = jnp.pad(per_slot, ((0, 0), (0, -per_slot.shape[1] % 128)))
        prefix, projection, all_slots = gather(
            levels,
            0,
            document_prefix_cache,
            out_proj,
            per_slot,
            shared=1 if lax.axis_size("group") == 2 else None,
        )
    else:
        prefix = lax.all_gather(document_prefix_cache, "line", axis=0, tiled=True)
        projection = lax.all_gather(out_proj, "line", axis=0, tiled=True)
        all_slots = lax.all_gather(per_slot, "line", axis=0, tiled=True)
    weight = lax.dynamic_slice_in_dim(all_slots, lax.axis_index("line"), 1, 1)
    mix = attend if small else attention
    context = mix(queries, question_key_values, prefix)
    attended = jnp.dot(context, projection, preferred_element_type=jnp.float32)
    mixture = residual_in.astype(jnp.float32) + attended
    normed = (
        mixture * lax.rsqrt(jnp.mean(mixture * mixture, axis=-1, keepdims=True) + 1e-06) * norm_gain
    ).astype(jnp.bfloat16)
    if small:
        (rows,) = gather(levels, 1, normed)
    else:
        rows = lax.all_gather(normed, "line", axis=0, tiled=True)
    share = run_expert(rows, weight, expert_gate, expert_up, expert_down)
    if small:
        summed = scatter(levels, 2, share)
    else:
        summed = lax.psum_scatter(share, "line", scatter_dimension=0, tiled=True)
    return (mixture + summed.astype(jnp.float32)).astype(jnp.bfloat16)


def solution(mesh):
    rows = P(("group", "line"), None)
    expert = P("line", None, None)
    placed = (rows, rows, rows, rows, P("line", None), P(), rows, rows, rows, P())
    return jax.shard_map(
        body,
        mesh=mesh,
        in_specs=placed + (expert, expert, expert),
        out_specs=rows,
        check_vma=False,
    )
```

```python
import functools
import math

import jax
import jax.numpy as jnp
from jax import lax
from jax.experimental import pallas as pl
from jax.experimental.pallas import tpu as pltpu
from jax.sharding import PartitionSpec as P

QUERY_HEADS = 16
KEY_VALUE_HEADS = 2
HEAD_SIZE = 128
QLEN = 16


MESH = pl.DeviceIdType.MESH
PLANE = 4


def place(levels, pair=False):
    line = lax.axis_index("line")
    group = lax.axis_index("group")
    level, side, core = line // PLANE, (line // 2) % 2, line % 2

    def device(level, side, core):
        return (group, level * PLANE + side * 2 + core)

    barrier = pltpu.get_barrier_semaphore()
    has_up, has_down = level + 1 < levels, level > 0

    def greet(target):
        pl.semaphore_signal(barrier, inc=1, device_id=target, device_id_type=MESH)

    if pair:
        greet((1 - group, line))
    extra = 1 if pair else 0
    greet(device(level, 1 - side, core))
    greet(device(level, side, 1 - core))
    pl.when(has_up)(lambda: greet(device(level + 1, side, core)))
    pl.when(has_down)(lambda: greet(device(level - 1, side, core)))
    inner = has_up & has_down
    pl.when(inner)(lambda: pl.semaphore_wait(barrier, 4 + extra))
    pl.when(jnp.logical_not(inner))(lambda: pl.semaphore_wait(barrier, 3 + extra))
    return level, side, core, device, has_up, has_down


def run_if(condition, action):
    if condition is None:
        action()
    else:
        pl.when(condition)(action)


def both(first, second):
    return second if first is None else first & second


def gather_kernel(levels, arrays, shared, *refs):
    ins, outs = refs[:arrays], refs[arrays : 2 * arrays]
    up_sem, down_sem, side_sem, core_sem, recv_sem, own_sem = refs[2 * arrays : 2 * arrays + 6]
    pair_send, pair_core, pair_recv = refs[2 * arrays + 6 :]
    level, side, core, device, has_up, has_down = place(levels, shared is not None)
    group = lax.axis_index("group")
    peer = (1 - group, lax.axis_index("line"))
    above, below = device(level + 1, side, core), device(level - 1, side, core)
    across, twin = device(level, 1 - side, core), device(level, side, 1 - core)
    pending = []

    def slot_of(at_level, at_side, at_core):
        return at_level * PLANE + at_side * 2 + at_core

    def part_of(array, ref, which):
        if which is None:
            return ref
        half = ins[array].shape[0] // 2
        return ref.at[pl.ds(pl.multiple_of(which * half, half), half)]

    def send(array, slot, source, target, sem, condition, which=None, recv=None):
        copy = pltpu.make_async_remote_copy(
            src_ref=part_of(array, source, which),
            dst_ref=part_of(array, outs[array].at[slot], which),
            send_sem=sem,
            recv_sem=recv_sem.at[array, slot] if recv is None else recv,
            device_id=target,
            device_id_type=MESH,
        )
        run_if(condition, copy.start)
        pending.append((condition, copy))

    def half_of(array):
        return group if array == shared else None

    def arrived(array, slot, condition, which=None, recv=None):
        landing = part_of(array, outs[array].at[slot], which)
        copy = pltpu.make_async_remote_copy(
            src_ref=landing,
            dst_ref=landing,
            send_sem=own_sem.at[array],
            recv_sem=recv_sem.at[array, slot] if recv is None else recv,
            device_id=twin,
            device_id_type=MESH,
        )
        run_if(condition, copy.wait_recv)

    mine = slot_of(level, side, core)
    own = []
    for array in range(arrays):
        source = ins[array]
        send(array, mine, source, above, up_sem.at[array, 0], has_up)
        send(array, mine, source, below, down_sem.at[array, 0], has_down)
        send(array, mine, source, across, side_sem.at[array, 0], None, half_of(array))
        send(array, mine, source, twin, core_sem.at[array, 0], None)
        copy = pltpu.make_async_copy(source, outs[array].at[mine], own_sem.at[array])
        copy.start()
        own.append(copy)
    for hop in range(1, levels):
        for array in range(arrays):
            there = level - hop >= 0
            slot = slot_of(level - hop, side, core)
            source = outs[array].at[slot]
            arrived(array, slot, there)
            send(array, slot, source, above, up_sem.at[array, hop], there & has_up)
            send(array, slot, source, across, side_sem.at[array, 2 * hop - 1], there, half_of(array))
            send(array, slot, source, twin, core_sem.at[array, 2 * hop - 1], there)
            there = level + hop < levels
            slot = slot_of(level + hop, side, core)
            source = outs[array].at[slot]
            arrived(array, slot, there)
            send(array, slot, source, below, down_sem.at[array, hop], there & has_down)
            send(array, slot, source, across, side_sem.at[array, 2 * hop], there, half_of(array))
            send(array, slot, source, twin, core_sem.at[array, 2 * hop], there)
    base = 2 * levels
    for stage in range(2):
        for hop in range(levels):
            for array in range(arrays):
                if stage == 1 and array != shared:
                    continue
                for sign in (-1, 1) if hop else (1,):
                    at_level = level + sign * hop
                    there = (at_level >= 0) & (at_level < levels) if hop else None
                    slot = slot_of(at_level, 1 - side, core)
                    index = 2 * hop + (sign + 1) // 2
                    source = outs[array].at[slot]
                    if stage == 0:
                        half = half_of(array)
                        arrived(array, slot, there, half)
                        if array == shared:
                            send(
                                array,
                                slot,
                                source,
                                peer,
                                pair_send.at[index],
                                there,
                                half,
                                pair_recv.at[slot],
                            )
                        sem = core_sem.at[array, base + index]
                        send(array, slot, source, twin, sem, there, half)
                    else:
                        half = 1 - group
                        arrived(array, slot, there, half, pair_recv.at[slot])
                        sem = pair_core.at[index]
                        send(array, slot, source, twin, sem, there, half, pair_recv.at[slot])
    for array in range(arrays):
        for at_level in range(levels):
            arrived(array, slot_of(at_level, side, 1 - core), None)
            slot = slot_of(at_level, 1 - side, 1 - core)
            arrived(array, slot, None, half_of(array))
            if array == shared:
                arrived(array, slot, None, 1 - group, pair_recv.at[slot])
        own[array].wait()
    for condition, copy in pending:
        run_if(condition, copy.wait_send)


def gather(levels, identity, *arrays, shared=None):
    count = len(arrays)
    devices = levels * PLANE
    sem = pltpu.SemaphoreType.DMA
    anywhere = pl.BlockSpec(memory_space=pl.ANY)
    outs = pl.pallas_call(
        functools.partial(gather_kernel, levels, count, shared),
        out_shape=[jax.ShapeDtypeStruct((devices,) + a.shape, a.dtype) for a in arrays],
        in_specs=[anywhere] * count,
        out_specs=[anywhere] * count,
        scratch_shapes=[
            sem((count, levels)),
            sem((count, levels)),
            sem((count, 2 * levels)),
            sem((count, 4 * levels)),
            sem((count, devices)),
            sem((count,)),
            sem((2 * levels,)),
            sem((2 * levels,)),
            sem((devices,)),
        ],
        compiler_params=pltpu.CompilerParams(collective_id=identity, has_side_effects=True),
    )(*arrays)
    return [out.reshape((-1, out.shape[-1])) for out in outs]


def scatter_kernel(
    levels,
    share,
    out,
    core_in,
    side_in,
    up_in,
    down_in,
    side_out,
    z_out,
    core_send,
    core_recv,
    side_send,
    side_recv,
    z_send,
    up_recv,
    down_recv,
):
    level, side, core, device, has_up, has_down = place(levels)
    above, below = device(level + 1, side, core), device(level - 1, side, core)
    across, twin = device(level, 1 - side, core), device(level, side, 1 - core)
    wide = jnp.float32

    def copy(source, landing, sem, recv, target):
        return pltpu.make_async_remote_copy(
            src_ref=source,
            dst_ref=landing,
            send_sem=sem,
            recv_sem=recv,
            device_id=target,
            device_id_type=MESH,
        )

    order = []
    for step in range(levels // 2):
        order += [levels - 1 - step, step]
    pending = []
    core_copies = {}
    for far in (1, 0):
        for at in order:
            at_side = 1 - side if far else side
            block = share.at[at * PLANE + at_side * 2 + (1 - core)]
            index = at * 2 + far
            one = copy(
                block, core_in.at[index], core_send.at[index], core_recv.at[index], twin
            )
            one.start()
            pending.append((None, one))
            core_copies[index] = one
    side_copies = {}
    for at in order:
        core_copies[at * 2 + 1].wait_recv()
        slot = at * PLANE + (1 - side) * 2 + core
        side_out[at] = (share[slot].astype(wide) + core_in[at * 2 + 1].astype(wide)).astype(
            side_out.dtype
        )
        one = copy(side_out.at[at], side_in.at[at], side_send.at[at], side_recv.at[at], across)
        one.start()
        pending.append((None, one))
        side_copies[at] = one
    for at in order:
        core_copies[at * 2].wait_recv()
        side_copies[at].wait_recv()
        up = copy(z_out.at[at], up_in.at[at], z_send.at[at], up_recv.at[at], above)
        down = copy(z_out.at[at], down_in.at[at], z_send.at[at], down_recv.at[at], below)

        def local(at=at):
            slot = at * PLANE + side * 2 + core
            return (
                share[slot].astype(wide)
                + core_in[at * 2].astype(wide)
                + side_in[at].astype(wide)
            )

        def start(value, one, at=at):
            z_out[at] = value.astype(z_out.dtype)
            one.start()

        def climb(at=at, up=up, local=local, start=start):
            up.wait_recv()
            start(local() + up_in[at].astype(wide), up)

        def drop(at=at, down=down, local=local, start=start):
            down.wait_recv()
            start(local() + down_in[at].astype(wide), down)

        def keep(local=local):
            out[...] = local()

        pl.when((at > level) & has_down)(climb)
        pl.when((at > level) & (level == 0))(lambda: start(local(), up))
        pl.when((at < level) & has_up)(drop)
        pl.when((at < level) & (level == levels - 1))(lambda: start(local(), down))
        pl.when(at == level)(keep)
        pending.append((at > level, up))
        pending.append((at < level, down))

    for at in range(levels):
        up = copy(z_out.at[at], up_in.at[at], z_send.at[at], up_recv.at[at], above)
        down = copy(z_out.at[at], down_in.at[at], z_send.at[at], down_recv.at[at], below)

        def take_up(at=at, up=up):
            up.wait_recv()
            out[...] += up_in[at].astype(wide)

        def take_down(at=at, down=down):
            down.wait_recv()
            out[...] += down_in[at].astype(wide)

        pl.when((at == level) & has_down)(take_up)
        pl.when((at == level) & has_up)(take_down)
    for condition, one in pending:
        run_if(condition, one.wait_send)


def scatter(levels, identity, share):
    devices = levels * PLANE
    rows, width = share.shape[0] // devices, share.shape[1]
    sem = pltpu.SemaphoreType.DMA
    block = (rows, width)
    vmem = pl.BlockSpec(memory_space=pltpu.VMEM)
    return pl.pallas_call(
        functools.partial(scatter_kernel, levels),
        out_shape=jax.ShapeDtypeStruct(block, jnp.float32),
        in_specs=[vmem],
        out_specs=vmem,
        scratch_shapes=[
            pltpu.VMEM((2 * levels,) + block, share.dtype),
            pltpu.VMEM((levels,) + block, share.dtype),
            pltpu.VMEM((levels,) + block, share.dtype),
            pltpu.VMEM((levels,) + block, share.dtype),
            pltpu.VMEM((levels,) + block, share.dtype),
            pltpu.VMEM((levels,) + block, share.dtype),
            sem((2 * levels,)),
            sem((2 * levels,)),
            sem((levels,)),
            sem((levels,)),
            sem((levels,)),
            sem((levels,)),
            sem((levels,)),
        ],
        compiler_params=pltpu.CompilerParams(
            collective_id=identity, has_side_effects=True, vmem_limit_bytes=40 * 1024 * 1024
        ),
    )(share.reshape((devices,) + block))


def attend_kernel(q_ref, key_ref, value_ref, near_key_ref, near_value_ref, out_ref):
    tokens = q_ref.shape[0]
    heads = q_ref.shape[1] // HEAD_SIZE
    scale = 1.0 / math.sqrt(HEAD_SIZE)
    q = jnp.concatenate(
        [q_ref[:, i * HEAD_SIZE : (i + 1) * HEAD_SIZE] for i in range(heads)], axis=0
    )
    dims = (((1,), (1,)), ((), ()))
    far = lax.dot_general(q, key_ref[...], dims, preferred_element_type=jnp.float32) * scale
    near = lax.dot_general(q, near_key_ref[...], dims, preferred_element_type=jnp.float32) * scale
    token = lax.rem(lax.broadcasted_iota(jnp.int32, near.shape, 0), tokens)
    other = lax.broadcasted_iota(jnp.int32, near.shape, 1)
    near = jnp.where((token // QLEN == other // QLEN) & (other <= token), near, -1e30)
    top = jnp.maximum(far.max(-1, keepdims=True), near.max(-1, keepdims=True))
    far = jnp.exp(far - top)
    near = jnp.exp(near - top)
    total = far.sum(-1, keepdims=True) + near.sum(-1, keepdims=True)
    acc = jnp.dot(far.astype(jnp.bfloat16), value_ref[...], preferred_element_type=jnp.float32)
    acc += jnp.dot(
        near.astype(jnp.bfloat16), near_value_ref[...], preferred_element_type=jnp.float32
    )
    context = (acc / total).astype(out_ref.dtype)
    for i in range(heads):
        out_ref[:, i * HEAD_SIZE : (i + 1) * HEAD_SIZE] = context[i * tokens : (i + 1) * tokens]


def attend(queries, local_kv, prefix):
    tokens, rows = queries.shape[0], prefix.shape[0]
    wide = 4 * HEAD_SIZE
    steps = QUERY_HEADS // KEY_VALUE_HEADS // 4
    return pl.pallas_call(
        attend_kernel,
        grid=(KEY_VALUE_HEADS, steps),
        out_shape=jax.ShapeDtypeStruct(queries.shape, queries.dtype),
        in_specs=[
            pl.BlockSpec((tokens, wide), lambda g, i: (0, g * steps + i)),
            pl.BlockSpec((rows, HEAD_SIZE), lambda g, i: (0, g)),
            pl.BlockSpec((rows, HEAD_SIZE), lambda g, i: (0, KEY_VALUE_HEADS + g)),
            pl.BlockSpec((tokens, HEAD_SIZE), lambda g, i: (0, g)),
            pl.BlockSpec((tokens, HEAD_SIZE), lambda g, i: (0, KEY_VALUE_HEADS + g)),
        ],
        out_specs=pl.BlockSpec((tokens, wide), lambda g, i: (0, g * steps + i)),
        compiler_params=pltpu.CompilerParams(vmem_limit_bytes=40 * 1024 * 1024),
    )(queries, prefix, prefix, local_kv, local_kv)


def expert_kernel(row_ref, weight_ref, gate_ref, up_ref, down_ref, out_ref):
    rows = row_ref[...]
    gate = jnp.dot(rows, gate_ref[0], preferred_element_type=jnp.float32)
    upper = jnp.dot(rows, up_ref[0], preferred_element_type=jnp.float32)
    middle = (gate / (1.0 + jnp.exp(-gate)) * upper).astype(jnp.bfloat16)
    answer = jnp.dot(middle, down_ref[0], preferred_element_type=jnp.float32)
    answer = answer.astype(jnp.bfloat16).astype(jnp.float32)
    out_ref[...] = (answer * weight_ref[...]).astype(out_ref.dtype)


def run_expert(rows, weight, gate, up, down):
    count, width = rows.shape
    block = math.gcd(count, 256)
    row_spec = pl.BlockSpec((block, width), lambda i: (i, 0))
    return pl.pallas_call(
        expert_kernel,
        grid=(count // block,),
        out_shape=jax.ShapeDtypeStruct(rows.shape, rows.dtype),
        in_specs=[
            row_spec,
            pl.BlockSpec((block, 1), lambda i: (i, 0)),
            pl.BlockSpec(gate.shape, lambda i: (0, 0, 0)),
            pl.BlockSpec(up.shape, lambda i: (0, 0, 0)),
            pl.BlockSpec(down.shape, lambda i: (0, 0, 0)),
        ],
        out_specs=row_spec,
        compiler_params=pltpu.CompilerParams(vmem_limit_bytes=48 * 1024 * 1024),
    )(rows, weight, gate, up, down)


def attention(queries, local_kv, prefix):
    tokens = queries.shape[0]
    group = QUERY_HEADS // KEY_VALUE_HEADS
    scale = 1.0 / math.sqrt(HEAD_SIZE)
    width = KEY_VALUE_HEADS * HEAD_SIZE
    heads = queries.reshape(tokens, KEY_VALUE_HEADS, group, HEAD_SIZE)
    near_k = local_kv[:, :width].reshape(tokens, KEY_VALUE_HEADS, HEAD_SIZE)
    near_v = local_kv[:, width:].reshape(tokens, KEY_VALUE_HEADS, HEAD_SIZE)
    near = (
        jnp.einsum("thgd,shd->thgs", heads, near_k, preferred_element_type=jnp.float32) * scale
    )
    position = jnp.arange(tokens, dtype=jnp.int32)
    visible = (position[:, None] // QLEN == position[None, :] // QLEN) & (
        position[None, :] <= position[:, None]
    )
    near = jnp.where(visible[:, None, None, :], near, -1e30)
    top = near.max(-1)
    terms = jnp.exp(near - top[..., None])
    total = terms.sum(-1)
    acc = jnp.einsum(
        "thgs,shd->thgd", terms.astype(jnp.bfloat16), near_v, preferred_element_type=jnp.float32
    )
    rows = prefix.shape[0]
    block = math.gcd(rows, 2048)

    def step(carry, piece):
        old_max, old_sum, old_acc = carry
        keys = piece[:, :width].reshape(block, KEY_VALUE_HEADS, HEAD_SIZE)
        values = piece[:, width:].reshape(block, KEY_VALUE_HEADS, HEAD_SIZE)
        far = jnp.einsum("thgd,nhd->thgn", heads, keys, preferred_element_type=jnp.float32) * scale
        new_max = jnp.maximum(old_max, far.max(-1))
        factor = jnp.exp(old_max - new_max)
        far = jnp.exp(far - new_max[..., None])
        new_acc = old_acc * factor[..., None] + jnp.einsum(
            "thgn,nhd->thgd", far.astype(jnp.bfloat16), values, preferred_element_type=jnp.float32
        )
        return (new_max, old_sum * factor + far.sum(-1), new_acc), None

    (top, total, acc), _ = lax.scan(
        step, (top, total, acc), prefix.reshape(rows // block, block, 2 * width)
    )
    return (acc / total[..., None]).reshape(tokens, QUERY_HEADS * HEAD_SIZE).astype(jnp.bfloat16)


def body(
    residual_in,
    queries,
    question_key_values,
    document_prefix_cache,
    out_proj,
    norm_gain,
    routes,
    keep_mask,
    route_weights,
    expert_slots,
    expert_gate,
    expert_up,
    expert_down,
):
    count = lax.axis_size("line")
    small = count % (2 * PLANE) == 0 and count * queries.shape[0] <= 2048
    levels = count // PLANE
    numbers = jnp.arange(expert_slots.shape[0], dtype=jnp.int32)
    slot_of_number = expert_slots[None, :] == numbers[:, None]
    number_of_slot = jnp.sum(jnp.where(slot_of_number, numbers[None, :], 0), axis=1)
    kept = jnp.where(keep_mask > 0, route_weights, 0.0)
    per_slot = jnp.sum(
        jnp.where(routes[:, :, None] == number_of_slot[None, None, :], kept[:, :, None], 0.0),
        axis=1,
    )
    if small:
        per_slot = jnp.pad(per_slot, ((0, 0), (0, -per_slot.shape[1] % 128)))
        prefix, projection, all_slots = gather(
            levels,
            0,
            document_prefix_cache,
            out_proj,
            per_slot,
        )
    else:
        prefix = lax.all_gather(document_prefix_cache, "line", axis=0, tiled=True)
        projection = lax.all_gather(out_proj, "line", axis=0, tiled=True)
        all_slots = lax.all_gather(per_slot, "line", axis=0, tiled=True)
    weight = lax.dynamic_slice_in_dim(all_slots, lax.axis_index("line"), 1, 1)
    mix = attend if small else attention
    context = mix(queries, question_key_values, prefix)
    attended = jnp.dot(context, projection, preferred_element_type=jnp.float32)
    mixture = residual_in.astype(jnp.float32) + attended
    normed = (
        mixture * lax.rsqrt(jnp.mean(mixture * mixture, axis=-1, keepdims=True) + 1e-06) * norm_gain
    ).astype(jnp.bfloat16)
    if small:
        (rows,) = gather(levels, 1, normed)
    else:
        rows = lax.all_gather(normed, "line", axis=0, tiled=True)
    share = run_expert(rows, weight, expert_gate, expert_up, expert_down)
    if small:
        summed = scatter(levels, 2, share)
    else:
        summed = lax.psum_scatter(share, "line", scatter_dimension=0, tiled=True)
    return (mixture + summed.astype(jnp.float32)).astype(jnp.bfloat16)


def solution(mesh):
    rows = P(("group", "line"), None)
    expert = P("line", None, None)
    placed = (rows, rows, rows, rows, P("line", None), P(), rows, rows, rows, P())
    return jax.shard_map(
        body,
        mesh=mesh,
        in_specs=placed + (expert, expert, expert),
        out_specs=rows,
        check_vma=False,
    )
```
